32 devices in a mesh: replica: 4 (over y, core), fsdp: 8 (over z, x).
Axes of the slice: x: 2, y: 2, z: 4, core: 2. Of those that a mesh axis runs over, the one named last changes fastest.
Arguments:
- anchor_params: bfloat16 [24, 512, 4096], P(None, 'fsdp')
- replica_params: bfloat16 [4, 24, 512, 4096], P('replica', None, 'fsdp')
- projection: bfloat16 [4096, 384], replicated
- momentum: float32 [24, 512, 384], P(None, 'fsdp'), may hold values from -1.8 to 1.8
- rate_table: float32 [4, 6], replicated, may hold values from 0.1 to 1
- owner_list: int32 [24], replicated, may hold values from 0 to 7, as said below
- layer_kind: int32 [24, 2], replicated, may hold values from 0 to 5, as said below
Outputs:
- new_params: bfloat16 [24, 512, 4096], P(None, 'fsdp')
- new_momentum: float32 [24, 512, 384], P(None, 'fsdp')
The draws below stay inside these ranges and needn't reach their ends.
Inputs may be any that keep to these rules, and one draw needn't show every extreme that they name: `owner_list`: no fsdp index is named more than 4 times, and in every draw some index is named exactly 4 times. `layer_kind`: column 0 is a layer, column 1 a kind below 6; each layer has 6 rows, and no two rows are equal.
All inputs are finite; a program needn't handle non-finite values.
Results may differ from the reference program's by a relative error of at most 0.0055.
Values may be sent and summed in bfloat16 or wider, within the bound.
A program may use at most 128 MiB of HBM per device.

```python
import math
import jax
import jax.numpy as jnp
from jax import lax

D = 4096
R = 384
ROWS = 512
MATS = 24
LAYERS = 4
KINDS = 6
OWN_MOST = 4
N_REPLICA = 4
N_FSDP = 8


def anchor_values(key):
    anchor_key = jax.random.fold_in(key, 1)
    values = jax.random.normal(anchor_key, (MATS, ROWS, D), jnp.float32)
    return values


def draw_anchor_params(key, part):
    return anchor_values(key).astype(jnp.bfloat16)


def draw_replica_params(key, part):
    anchor = anchor_values(key)
    row_key = jax.random.fold_in(key, 2)
    matrix_key = jax.random.fold_in(key, 3)
    noise_key = jax.random.fold_in(key, 4)
    row_scale = jnp.exp(jax.random.uniform(row_key, (MATS, ROWS), jnp.float32, 0.0, math.log(10.0)))
    ramp = 1.0 + 2.0 * jnp.arange(ROWS, dtype=jnp.float32) / max(ROWS - 1, 1)
    matrix_scale = jnp.exp(jax.random.uniform(matrix_key, (MATS,), jnp.float32, math.log(0.3), math.log(3.0)))
    spread = 0.02 * row_scale * ramp[None, :] * matrix_scale[:, None]
    noise = jax.random.normal(noise_key, (N_REPLICA, MATS, ROWS, D), jnp.float32)
    return (anchor[None] + noise * spread[None, :, :, None]).astype(jnp.bfloat16)


def draw_projection(key, part):
    value_key = jax.random.fold_in(key, 6)
    column_key = jax.random.fold_in(key, 7)
    column_scale = jnp.exp(jax.random.uniform(column_key, (R,), jnp.float32, 0.0, math.log(10.0)))
    values = jax.random.normal(value_key, (D, R), jnp.float32)
    return (values * column_scale[None, :] / math.sqrt(D)).astype(jnp.bfloat16)


def draw_owner_list(key, part):
    first_key = jax.random.fold_in(key, 20)
    rest_key = jax.random.fold_in(key, 21)
    order_key = jax.random.fold_in(key, 22)
    first = jax.random.randint(first_key, (), 0, N_FSDP)
    others = jax.random.permutation(rest_key, OWN_MOST * (N_FSDP - 1))[:MATS - OWN_MOST]
    rest = (first + 1 + others % (N_FSDP - 1)) % N_FSDP
    listed = jnp.concatenate([jnp.full((OWN_MOST,), first, jnp.int32), rest.astype(jnp.int32)])
    shifted = (listed + (N_FSDP - 1 - jnp.max(listed))) % N_FSDP
    order = jax.random.permutation(order_key, MATS)
    return shifted[order].astype(jnp.int32)


def draw_layer_kind(key, part):
    per_layer = MATS // LAYERS
    kind_parts = []
    for layer_index in range(LAYERS):
        layer_key = jax.random.fold_in(key, 40 + layer_index)
        if layer_index == 0:
            chosen = jnp.concatenate([jnp.full((1,), KINDS - 1, jnp.int32), jax.random.permutation(layer_key, KINDS - 1)[:per_layer - 1].astype(jnp.int32)])
        else:
            chosen = jax.random.permutation(layer_key, KINDS)[:per_layer].astype(jnp.int32)
        kind_parts.append(chosen)
    kinds = jnp.concatenate(kind_parts)
    layers = jnp.arange(MATS, dtype=jnp.int32) // per_layer
    table = jnp.stack([layers, kinds], axis=1)
    order = jax.random.permutation(jax.random.fold_in(key, 60), MATS)
    return table[order].astype(jnp.int32)


def block_levels(rng, shape, cuts, smallest, top_value):
    gain, own = 1.0, jax.random.fold_in(rng, 6)
    for dim, shards_of in cuts:
        draws = jnp.exp(jax.random.uniform(jax.random.fold_in(own, dim), (shards_of,), jnp.float32, smallest / len(cuts), top_value / len(cuts)))
        gain = gain * jnp.repeat(draws, shape[dim] // shards_of).reshape([-1 if axis == dim else 1 for axis in range(len(shape))])
    return gain


def scatter_about(key, extent, scale, most, pieces=(), kind=jnp.bfloat16):
    array = scale * jax.random.normal(key, extent, jnp.float32)
    if pieces:
        array = array * block_levels(key, extent, pieces, -0.22, 0.18)
    return jnp.clip(array, -most, most).astype(kind)


def setup_inputs(seed: int = 0) -> dict:
    arg_keys = jax.random.split(jax.random.key(seed), 8)
    return {
        "anchor_params": draw_anchor_params(jax.random.fold_in(arg_keys[7], 71), 0),
        "replica_params": draw_replica_params(jax.random.fold_in(arg_keys[7], 71), 0),
        "projection": draw_projection(jax.random.fold_in(arg_keys[7], 71), 0),
        "momentum": scatter_about(arg_keys[3], (MATS, ROWS, R), 0.3, 1.8, ((1, 8),), jnp.float32),
        "rate_table": jnp.clip(jnp.exp(jax.random.uniform(arg_keys[4], (LAYERS, KINDS), jnp.float32, math.log(0.1), math.log(1.0))), 0.1, 1.0),
        "owner_list": draw_owner_list(jax.random.fold_in(arg_keys[7], 71), 0),
        "layer_kind": draw_layer_kind(jax.random.fold_in(arg_keys[7], 71), 0),
    }


OUTER_MOMENTUM = 0.9
EPSILON = 1e-06

def reference(anchor_params, replica_params, projection, momentum, rate_table, owner_list, layer_kind):
    summed = jnp.zeros((MATS, ROWS, R), jnp.float32)
    for replica_index in range(N_REPLICA):
        pseudo_grad = (anchor_params.astype(jnp.float32) - replica_params[replica_index].astype(jnp.float32)).astype(jnp.bfloat16)
        compressed = jnp.dot(pseudo_grad.reshape(MATS * ROWS, D), projection, preferred_element_type=jnp.float32)
        summed = summed + compressed.reshape(MATS, ROWS, R)
    outer_grad = summed / N_REPLICA
    new_momentum = OUTER_MOMENTUM * momentum + outer_grad
    outer_step = outer_grad + OUTER_MOMENTUM * new_momentum
    squares = lax.optimization_barrier(jnp.sum(outer_step * outer_step, axis=(1, 2)))
    same_group = (owner_list[:, None] == owner_list[None, :]).astype(jnp.float32)
    group_squares = jnp.dot(same_group, squares, precision=lax.Precision.HIGHEST)
    group_count = lax.optimization_barrier(jnp.sum(same_group, axis=1))
    scaling = lax.rsqrt(group_squares / (group_count * (ROWS * R)) + EPSILON)
    outer_rate = rate_table[layer_kind[:, 0], layer_kind[:, 1]]
    direction = (outer_step * (outer_rate * scaling)[:, None, None]).astype(jnp.bfloat16)
    update = lax.dot_general(direction.reshape(MATS * ROWS, R), projection, (((1,), (1,)), ((), ())), preferred_element_type=jnp.float32).astype(jnp.bfloat16)
    new_params = (anchor_params.astype(jnp.float32) - update.reshape(MATS, ROWS, D).astype(jnp.float32)).astype(jnp.bfloat16)
    return (new_params, new_momentum)
```

```python
import jax
import jax.numpy as jnp
from jax import lax
from jax.sharding import PartitionSpec as P

OUTER_MOMENTUM = 0.9
EPSILON = 1e-06


def local(anchor_params, replica_params, projection, momentum, rate_table, owner_list, layer_kind):
    matrices, rows_dev, model_width = anchor_params.shape
    rank_dim = projection.shape[1]
    all_rows = rows_dev * lax.axis_size("fsdp")
    pseudo_grad = (
        anchor_params.astype(jnp.float32) - replica_params[0].astype(jnp.float32)
    ).astype(jnp.bfloat16)
    compressed = jnp.dot(
        pseudo_grad.reshape(matrices * rows_dev, model_width),
        projection,
        preferred_element_type=jnp.float32,
    )
    summed = lax.psum(compressed.reshape(matrices, rows_dev, rank_dim), "replica")
    outer_grad = summed / lax.axis_size("replica")
    new_momentum = OUTER_MOMENTUM * momentum + outer_grad
    outer_step = outer_grad + OUTER_MOMENTUM * new_momentum
    same_group = (owner_list[:, None] == owner_list[None, :]).astype(jnp.float32)
    outer_rate = rate_table[layer_kind[:, 0], layer_kind[:, 1]]
    squares = lax.psum(jnp.sum(outer_step * outer_step, axis=(1, 2)), "fsdp")
    group_squares = jnp.sum(same_group * squares[None, :], axis=1)
    group_count = jnp.sum(same_group, axis=1)
    scaling = lax.rsqrt(group_squares / (group_count * (all_rows * rank_dim)) + EPSILON)
    direction = (outer_step * (outer_rate * scaling)[:, None, None]).astype(jnp.bfloat16)
    update = lax.dot_general(
        direction.reshape(-1, rank_dim), projection, (((1,), (1,)), ((), ())),
        preferred_element_type=jnp.float32,
    ).astype(jnp.bfloat16).reshape(anchor_params.shape)
    new_params = (anchor_params.astype(jnp.float32) - update.astype(jnp.float32)).astype(
        jnp.bfloat16
    )
    return (new_params, new_momentum)


def solution(mesh):
    placed = (
        P(None, "fsdp", None),
        P("replica", None, "fsdp", None),
        P(),
        P(None, "fsdp", None),
        P(),
        P(),
        P(),
    )
    return jax.shard_map(
        local,
        mesh=mesh,
        in_specs=placed,
        out_specs=(P(None, "fsdp", None), P(None, "fsdp", None)),
        check_vma=False,
    )
```

```python
import functools
import jax
import jax.numpy as jnp
from jax import lax
from jax.experimental import pallas as pl
from jax.experimental.pallas import tpu as pltpu
from jax.sharding import PartitionSpec as P

OUTER_MOMENTUM = 0.9
EPSILON = 1e-06
CHUNKS = 6
CORES = 2
F32 = jnp.float32
BF16 = jnp.bfloat16


def reduce_kernel(matrices, n_replica, n_fsdp, *refs):
    (anchor, replica, proj, mom,
     anchor_v, proj_v, step_v, nm_v, sq_v,
     rep_v, mom_v, comp_v, prec_v, ys_v, og_v, sq_all,
     a_sem, r_sem, one_sem, p_send, p_recv, y_send, y_recv, q_send, q_recv, s_send, s_recv) = refs
    rows, width = anchor.shape
    rank = proj.shape[1]
    per = matrices // CHUNKS
    size = rows // CHUNKS
    half = size // CORES
    n_y = n_replica // CORES
    rep = lax.axis_index("replica")
    f = lax.axis_index("fsdp")
    y = rep // CORES
    core = rep % CORES
    partner = y * CORES + 1 - core

    def load(k):
        rs = pl.ds(k * size, size)
        return (pltpu.make_async_copy(anchor.at[rs], anchor_v.at[rs], a_sem.at[k]),
                pltpu.make_async_copy(replica.at[rs], rep_v.at[rs], r_sem.at[k]))

    pcopy = pltpu.make_async_copy(proj, proj_v, one_sem.at[0])
    mcopy = pltpu.make_async_copy(mom, mom_v, one_sem.at[1])
    pcopy.start()
    for k in range(2):
        for c in load(k):
            c.start()

    barrier = pltpu.get_barrier_semaphore()
    pl.semaphore_signal(barrier, inc=1, device_id={"replica": partner})
    for d in range(1, n_y):
        pl.semaphore_signal(barrier, inc=1, device_id={"replica": lax.rem(y + d, n_y) * CORES + core})
    for d in range(1, n_fsdp):
        pl.semaphore_signal(barrier, inc=1, device_id={"fsdp": lax.rem(f + d, n_fsdp)})

    mine = pl.multiple_of(core * half, half)
    theirs = pl.multiple_of((1 - core) * half, half)

    def p_copy(k):
        return pltpu.make_async_remote_copy(
            comp_v.at[k, pl.ds(theirs, half)], prec_v.at[k], p_send.at[k], p_recv.at[k],
            device_id={"replica": partner})

    def y_copy(k, d, slot):
        return pltpu.make_async_remote_copy(
            ys_v.at[slot, k], ys_v.at[slot, k], y_send.at[d - 1, k], y_recv.at[d - 1, k],
            device_id={"replica": lax.rem(y + d, n_y) * CORES + core})

    def q_copy(k, off):
        return pltpu.make_async_remote_copy(
            og_v.at[k, pl.ds(off, half)], og_v.at[k, pl.ds(off, half)], q_send.at[k], q_recv.at[k],
            device_id={"replica": partner})

    def s_copy(d, slot):
        return pltpu.make_async_remote_copy(
            sq_all.at[slot], sq_all.at[slot], s_send.at[d - 1], s_recv.at[d - 1],
            device_id={"fsdp": lax.rem(f + d, n_fsdp)})

    def stage_a(k):
        if k == 0:
            pcopy.wait()
        for c in load(k):
            c.wait()
        if k + 2 < CHUNKS:
            for c in load(k + 2):
                c.start()
        if k + 2 == CHUNKS:
            mcopy.start()
        rs = pl.ds(k * size, size)
        pseudo = (anchor_v[rs, :].astype(F32) - rep_v[rs, :].astype(F32)).astype(BF16)
        comp_v[k] = jnp.dot(pseudo, proj_v[...], preferred_element_type=F32)
        if k == 0:
            pl.semaphore_wait(barrier, 1 + (n_y - 1) + (n_fsdp - 1))
        p_copy(k).start()

    def stage_b(k):
        p_copy(k).wait_recv()
        ys_v[y, k] = (comp_v[k, pl.ds(mine, half)] + prec_v[k]).astype(BF16)
        for d in range(1, n_y):
            y_copy(k, d, y).start()

    def stage_c(k):
        for d in range(1, n_y):
            y_copy(k, d, lax.rem(y + n_y - d, n_y)).wait_recv()
        total = ys_v[0, k].astype(F32)
        for i in range(1, n_y):
            total = total + ys_v[i, k].astype(F32)
        og_v[k, pl.ds(mine, half)] = total * (1.0 / n_replica)
        q_copy(k, mine).start()

    def stage_d(k):
        if k == 0:
            mcopy.wait()
        q_copy(k, theirs).wait_recv()
        rs = pl.ds(k * size, size)
        grad = og_v[k]
        moved = OUTER_MOMENTUM * mom_v[rs, :] + grad
        nm_v[rs, :] = moved
        step = grad + OUTER_MOMENTUM * moved
        step_v[rs, :] = step
        square = jnp.sum((step * step).reshape(per, rows // matrices, rank), axis=1)
        lanes = square[:, :128]
        for i in range(1, rank // 128):
            lanes = lanes + square[:, i * 128:(i + 1) * 128]
        sq_all[f, pl.ds(k * per, per), :] = lanes

    for k in range(CHUNKS + 1):
        if k < CHUNKS:
            stage_a(k)
        if k >= 1:
            stage_b(k - 1)
    for k in range(CHUNKS + 1):
        if k < CHUNKS:
            stage_c(k)
        if k >= 1:
            stage_d(k - 1)
    for d in range(1, n_fsdp):
        s_copy(d, f).start()
    for k in range(CHUNKS):
        p_copy(k).wait_send()
        for d in range(1, n_y):
            y_copy(k, d, y).wait_send()
        q_copy(k, mine).wait_send()
    for d in range(1, n_fsdp):
        s_copy(d, lax.rem(f + n_fsdp - d, n_fsdp)).wait_recv()
    total = sq_all[0]
    for i in range(1, n_fsdp):
        total = total + sq_all[i]
    sq_v[...] = total
    for d in range(1, n_fsdp):
        s_copy(d, f).wait_send()


def apply_kernel(matrices, entries, anchor_v, proj_v, step_v, nm_v, sq_v, rates, owners, kinds,
                 new_params, new_mom, out_v, fac_v, o_sem, m_sem):
    rows, width = anchor_v.shape
    rank = proj_v.shape[1]
    mcopy = pltpu.make_async_copy(nm_v, new_mom, m_sem)
    mcopy.start()
    lane = sq_v.shape[1]
    index = lax.broadcasted_iota(jnp.int32, (matrices, lane), 0)
    owner = jnp.zeros((matrices, lane), jnp.int32)
    rate = jnp.zeros((matrices, lane), F32)
    for m in range(matrices):
        owner = jnp.where(index == m, owners[m], owner)
        rate = jnp.where(index == m, rates[kinds[m, 0], kinds[m, 1]], rate)
    group = jnp.zeros((matrices, lane), F32)
    count = jnp.zeros((matrices, lane), F32)
    for m in range(matrices):
        same = owner == owners[m]
        group = group + jnp.where(same, sq_v[pl.ds(m, 1), :], 0.0)
        count = count + jnp.where(same, 1.0, 0.0)
    group = jnp.sum(group, axis=1, keepdims=True)
    fac_v[...] = rate * lax.rsqrt(group / (count * entries) + EPSILON)
    per = matrices // CHUNKS
    each = rows // matrices
    size = rows // CHUNKS

    def out_copy(k):
        return pltpu.make_async_copy(out_v.at[k % 2], new_params.at[pl.ds(k * size, size)], o_sem.at[k % 2])

    tile = 1024
    for k in range(CHUNKS):
        if k >= 2:
            out_copy(k - 2).wait()
        parts = []
        for i in range(per):
            m = k * per + i
            parts.append(step_v[pl.ds(m * each, each), :] * fac_v[pl.ds(m, 1), 0:1])
        direction = jnp.concatenate(parts, axis=0).astype(BF16)
        for j in range(width // tile):
            cs = pl.ds(j * tile, tile)
            update = lax.dot_general(direction, proj_v[cs, :], (((1,), (1,)), ((), ())),
                                     preferred_element_type=F32).astype(BF16)
            out_v[k % 2, :, cs] = (anchor_v[pl.ds(k * size, size), cs].astype(F32)
                                   - update.astype(F32)).astype(BF16)
        out_copy(k).start()
    for k in range(CHUNKS - 2, CHUNKS):
        out_copy(k).wait()
    mcopy.wait()


def local(anchor_params, replica_params, projection, momentum, rate_table, owner_list, layer_kind):
    matrices, rows_dev, width = anchor_params.shape
    rank = projection.shape[1]
    n_replica = lax.axis_size("replica")
    n_fsdp = lax.axis_size("fsdp")
    n_y = n_replica // CORES
    rows = matrices * rows_dev
    size = rows // CHUNKS
    half = size // CORES
    anchor = anchor_params.reshape(rows, width)
    replica = replica_params.reshape(rows, width)
    any_spec = pl.BlockSpec(memory_space=pl.ANY)
    vmem = pl.BlockSpec(memory_space=pltpu.VMEM)
    smem = pl.BlockSpec(memory_space=pltpu.SMEM)
    dma = pltpu.SemaphoreType.DMA
    held = pl.pallas_call(
        functools.partial(reduce_kernel, matrices, n_replica, n_fsdp),
        out_shape=(
            pltpu.VMEM((rows, width), BF16),
            pltpu.VMEM((width, rank), BF16),
            pltpu.VMEM((rows, rank), F32),
            pltpu.VMEM((rows, rank), F32),
            pltpu.VMEM((matrices, 128), F32),
        ),
        in_specs=[any_spec] * 4,
        out_specs=(vmem,) * 5,
        scratch_shapes=[
            pltpu.VMEM((rows, width), BF16),
            pltpu.VMEM((rows, rank), F32),
            pltpu.VMEM((CHUNKS, size, rank), F32),
            pltpu.VMEM((CHUNKS, half, rank), F32),
            pltpu.VMEM((n_y, CHUNKS, half, rank), BF16),
            pltpu.VMEM((CHUNKS, size, rank), F32),
            pltpu.VMEM((n_fsdp, matrices, 128), F32),
            dma((CHUNKS,)), dma((CHUNKS,)), dma((2,)),
            dma((CHUNKS,)), dma((CHUNKS,)),
            dma((n_y - 1, CHUNKS)), dma((n_y - 1, CHUNKS)),
            dma((CHUNKS,)), dma((CHUNKS,)),
            dma((n_fsdp - 1,)), dma((n_fsdp - 1,)),
        ],
        compiler_params=pltpu.CompilerParams(
            collective_id=0, has_side_effects=True, vmem_limit_bytes=32 * 1024 * 1024),
    )(anchor, replica, projection, momentum.reshape(rows, rank))
    new_params, new_mom = pl.pallas_call(
        functools.partial(apply_kernel, matrices, float(rows_dev * n_fsdp * rank)),
        out_shape=(
            jax.ShapeDtypeStruct((rows, width), BF16),
            jax.ShapeDtypeStruct((rows, rank), F32),
        ),
        in_specs=[vmem] * 5 + [smem] * 3,
        out_specs=(any_spec, any_spec),
        scratch_shapes=[
            pltpu.VMEM((2, size, width), BF16),
            pltpu.VMEM((matrices, 128), F32),
            dma((2,)), dma(()),
        ],
        compiler_params=pltpu.CompilerParams(vmem_limit_bytes=24 * 1024 * 1024),
    )(*held, rate_table, owner_list, layer_kind)
    return new_params.reshape(anchor_params.shape), new_mom.reshape(momentum.shape)


def solution(mesh):
    placed = (
        P(None, "fsdp", None),
        P("replica", None, "fsdp", None),
        P(),
        P(None, "fsdp", None),
        P(),
        P(),
        P(),
    )
    return jax.shard_map(
        local,
        mesh=mesh,
        in_specs=placed,
        out_specs=(P(None, "fsdp", None), P(None, "fsdp", None)),
        check_vma=False,
    )
```

```python
import functools
import jax
import jax.numpy as jnp
from jax import lax
from jax.experimental import pallas as pl
from jax.experimental.pallas import tpu as pltpu
from jax.sharding import PartitionSpec as P

OUTER_MOMENTUM = 0.9
EPSILON = 1e-06
CHUNKS = 6
CORES = 2
EARLY = 1
LAG = 5
RING = 3
TILE = 1024
F32 = jnp.float32
BF16 = jnp.bfloat16


def reduce_kernel(matrices, n_replica, n_fsdp, *refs):
    (anchor, replica, proj, mom,
     anchor_v, proj_v, early_v, step_v, nm_v, sq_v,
     rep_v, mom_v, comp_v, prec_v, ys_v, og_v, st_v, sq_all,
     a_sem, r_sem, one_sem, p_send, p_recv, y_send, y_recv, q_send, q_recv, s_send, s_recv) = refs
    rows, width = anchor.shape
    rank = proj.shape[1]
    per = matrices // CHUNKS
    size = rows // CHUNKS
    half = size // CORES
    n_y = n_replica // CORES
    rep = lax.axis_index("replica")
    f = lax.axis_index("fsdp")
    y = rep // CORES
    core = rep % CORES
    partner = y * CORES + 1 - core

    def span(k):
        return pl.ds(pl.multiple_of(k * size, size), size)

    def load(k):
        return (pltpu.make_async_copy(anchor.at[span(k)], anchor_v.at[span(k)], a_sem.at[k]),
                pltpu.make_async_copy(replica.at[span(k)], rep_v.at[k % RING], r_sem.at[k]))

    pcopy = pltpu.make_async_copy(proj, proj_v, one_sem.at[0])
    mcopy = pltpu.make_async_copy(mom, mom_v, one_sem.at[1])
    pcopy.start()
    for k in range(RING - 1):
        for c in load(k):
            c.start()

    barrier = pltpu.get_barrier_semaphore()
    pl.semaphore_signal(barrier, inc=1, device_id={"replica": partner})
    for d in range(1, n_y):
        pl.semaphore_signal(barrier, inc=1, device_id={"replica": lax.rem(y + d, n_y) * CORES + core})
    for d in range(1, n_fsdp):
        pl.semaphore_signal(barrier, inc=1, device_id={"fsdp": lax.rem(f + d, n_fsdp)})

    mine = pl.multiple_of(core * half, half)
    theirs = pl.multiple_of((1 - core) * half, half)

    def p_copy(k):
        return pltpu.make_async_remote_copy(
            comp_v.at[k, pl.ds(theirs, half)], prec_v.at[k], p_send.at[k], p_recv.at[k],
            device_id={"replica": partner})

    def y_copy(k, d, slot):
        return pltpu.make_async_remote_copy(
            ys_v.at[slot, k], ys_v.at[slot, k], y_send.at[d - 1, k], y_recv.at[d - 1, k],
            device_id={"replica": lax.rem(y + d, n_y) * CORES + core})

    def q_copy(k, off):
        return pltpu.make_async_remote_copy(
            og_v.at[k, pl.ds(off, half)], og_v.at[k, pl.ds(off, half)], q_send.at[k], q_recv.at[k],
            device_id={"replica": partner})

    def s_copy(d, slot):
        return pltpu.make_async_remote_copy(
            sq_all.at[slot], sq_all.at[slot], s_send.at[d - 1], s_recv.at[d - 1],
            device_id={"fsdp": lax.rem(f + d, n_fsdp)})

    def stage_a(k):
        for c in load(k):
            c.wait()

        @pl.when(k + RING - 1 < CHUNKS)
        def _():
            for c in load(k + RING - 1):
                c.start()

        pseudo = anchor_v[span(k), :] - rep_v[k % RING]
        comp_v[k] = jnp.dot(pseudo, proj_v[...], preferred_element_type=F32)
        p_copy(k).start()

    def stage_b(k):
        p_copy(k).wait_recv()
        ys_v[y, k] = (comp_v[k, pl.ds(mine, half)] + prec_v[k]).astype(BF16)
        for d in range(1, n_y):
            y_copy(k, d, y).start()

    def stage_c(k):
        for d in range(1, n_y):
            y_copy(k, d, lax.rem(y + n_y - d, n_y)).wait_recv()
        total = ys_v[0, k].astype(F32)
        for i in range(1, n_y):
            total = total + ys_v[i, k].astype(F32)
        og_v[k, pl.ds(mine, half)] = total * (1.0 / n_replica)
        q_copy(k, mine).start()

    def stage_d(k):
        q_copy(k, theirs).wait_recv()
        grad = og_v[k]
        moved = OUTER_MOMENTUM * mom_v[span(k), :] + grad
        nm_v[span(k), :] = moved
        step = grad + OUTER_MOMENTUM * moved

        @pl.when(k < EARLY)
        def _():
            st_v[jnp.minimum(k, EARLY - 1)] = step.astype(BF16)

        @pl.when(k >= EARLY)
        def _():
            step_v[jnp.maximum(k - EARLY, 0)] = step

        square = jnp.sum((step * step).reshape(per, rows // matrices, rank), axis=1)
        lanes = square[:, :128]
        for i in range(1, rank // 128):
            lanes = lanes + square[:, i * 128:(i + 1) * 128]
        sq_all[f, k] = lanes

    def stage_e(k):
        for j in range(width // TILE):
            cs = pl.ds(j * TILE, TILE)
            early_v[span(k), cs] = lax.dot_general(
                st_v[k], proj_v[cs, :], (((1,), (1,)), ((), ())), preferred_element_type=F32)

    pcopy.wait()
    pl.semaphore_wait(barrier, 1 + (n_y - 1) + (n_fsdp - 1))

    def first(k, _):
        stage_a(k)

        @pl.when(k >= 1)
        def _():
            stage_b(k - 1)

        @pl.when(k == 1)
        def _():
            mcopy.start()

        @pl.when(k == LAG)
        def _():
            mcopy.wait()

        @pl.when(k >= LAG)
        def _():
            stage_c(k - LAG)

        @pl.when(k > LAG)
        def _():
            stage_d(k - LAG - 1)

    lax.fori_loop(0, CHUNKS, first, None)
    stage_b(CHUNKS - 1)

    def second(k, _):
        stage_c(k)
        stage_d(k - 1)

    lax.fori_loop(CHUNKS - LAG, CHUNKS, second, None)
    stage_d(CHUNKS - 1)
    for d in range(1, n_fsdp):
        s_copy(d, f).start()

    def third(k, _):
        stage_e(k)

    lax.fori_loop(0, EARLY, third, None)
    for k in range(CHUNKS):
        p_copy(k).wait_send()
        for d in range(1, n_y):
            y_copy(k, d, y).wait_send()
        q_copy(k, mine).wait_send()
    for d in range(1, n_fsdp):
        s_copy(d, lax.rem(f + n_fsdp - d, n_fsdp)).wait_recv()
    total = sq_all[0]
    for i in range(1, n_fsdp):
        total = total + sq_all[i]
    sq_v[...] = total
    for d in range(1, n_fsdp):
        s_copy(d, f).wait_send()


def apply_kernel(matrices, entries, anchor_v, proj_v, early_v, step_v, nm_v, sq_v, rates, owners,
                 kinds, new_params, new_mom, out_v, fac_v, o_sem, m_sem):
    rows, width = anchor_v.shape
    per = matrices // CHUNKS
    each = rows // matrices
    size = rows // CHUNKS
    lane = 128
    mcopy = pltpu.make_async_copy(nm_v, new_mom, m_sem)
    index = lax.broadcasted_iota(jnp.int32, (matrices, lane), 0)
    owner = jnp.zeros((matrices, lane), jnp.int32)
    rate = jnp.zeros((matrices, lane), F32)
    for m in range(matrices):
        owner = jnp.where(index == m, owners[m], owner)
        rate = jnp.where(index == m, rates[kinds[0, m], kinds[1, m]], rate)
    group = jnp.zeros((matrices, lane), F32)
    count = jnp.zeros((matrices, lane), F32)
    for m in range(matrices):
        same = owner == owners[m]
        group = group + jnp.where(same, sq_v[m // per, pl.ds(m % per, 1), :], 0.0)
        count = count + jnp.where(same, 1.0, 0.0)
    group = jnp.sum(group, axis=1, keepdims=True)
    fac_v[...] = rate * lax.rsqrt(group / (count * entries) + EPSILON)

    def out_copy(k):
        rs = pl.ds(pl.multiple_of(k * size, size), size)
        return pltpu.make_async_copy(out_v.at[k % 3], new_params.at[rs], o_sem.at[k % 3])

    def turn(k):
        @pl.when(k >= 3)
        def _():
            out_copy(k - 3).wait()

    def early(k, _):
        turn(k)

        def one(i, _):
            m = k * per + i
            rs = pl.ds(pl.multiple_of(m * each, each), each)
            factor = fac_v[pl.ds(m, 1), 0:1]
            update = (early_v[rs, :] * factor).astype(BF16)
            out_v[k % 3, pl.ds(pl.multiple_of(i * each, each), each), :] = anchor_v[rs, :] - update

        lax.fori_loop(0, per, one, None)
        out_copy(k).start()

    def late(k, _):
        turn(k)
        parts = []
        for i in range(per):
            parts.append(step_v[k - EARLY, i * each:(i + 1) * each, :]
                         * fac_v[pl.ds(k * per + i, 1), 0:1])
        direction = jnp.concatenate(parts, axis=0).astype(BF16)
        for j in range(width // TILE):
            cs = pl.ds(j * TILE, TILE)
            update = lax.dot_general(direction, proj_v[cs, :], (((1,), (1,)), ((), ())),
                                     preferred_element_type=F32).astype(BF16)
            rs = pl.ds(pl.multiple_of(k * size, size), size)
            out_v[k % 3, :, cs] = anchor_v[rs, cs] - update
        out_copy(k).start()

    lax.fori_loop(0, EARLY, early, None)
    mcopy.start()
    lax.fori_loop(EARLY, CHUNKS, late, None)
    for k in range(CHUNKS - 3, CHUNKS):
        out_copy(k).wait()
    mcopy.wait()


def local(anchor_params, replica_params, projection, momentum, rate_table, owner_list, layer_kind):
    matrices, rows_dev, width = anchor_params.shape
    rank = projection.shape[1]
    n_replica = lax.axis_size("replica")
    n_fsdp = lax.axis_size("fsdp")
    n_y = n_replica // CORES
    rows = matrices * rows_dev
    size = rows // CHUNKS
    half = size // CORES
    anchor = anchor_params.reshape(rows, width)
    replica = replica_params.reshape(rows, width)
    any_spec = pl.BlockSpec(memory_space=pl.ANY)
    vmem = pl.BlockSpec(memory_space=pltpu.VMEM)
    smem = pl.BlockSpec(memory_space=pltpu.SMEM)
    dma = pltpu.SemaphoreType.DMA
    held = pl.pallas_call(
        functools.partial(reduce_kernel, matrices, n_replica, n_fsdp),
        out_shape=(
            pltpu.VMEM((rows, width), BF16),
            pltpu.VMEM((width, rank), BF16),
            pltpu.VMEM((EARLY * size, width), F32),
            pltpu.VMEM((CHUNKS - EARLY, size, rank), F32),
            pltpu.VMEM((rows, rank), F32),
            pltpu.VMEM((CHUNKS, matrices // CHUNKS, 128), F32),
        ),
        in_specs=[any_spec] * 4,
        out_specs=(vmem,) * 6,
        scratch_shapes=[
            pltpu.VMEM((RING, size, width), BF16),
            pltpu.VMEM((rows, rank), F32),
            pltpu.VMEM((CHUNKS, size, rank), F32),
            pltpu.VMEM((CHUNKS, half, rank), F32),
            pltpu.VMEM((n_y, CHUNKS, half, rank), BF16),
            pltpu.VMEM((CHUNKS, size, rank), F32),
            pltpu.VMEM((EARLY, size, rank), BF16),
            pltpu.VMEM((n_fsdp, CHUNKS, matrices // CHUNKS, 128), F32),
            dma((CHUNKS,)), dma((CHUNKS,)), dma((2,)),
            dma((CHUNKS,)), dma((CHUNKS,)),
            dma((n_y - 1, CHUNKS)), dma((n_y - 1, CHUNKS)),
            dma((CHUNKS,)), dma((CHUNKS,)),
            dma((n_fsdp - 1,)), dma((n_fsdp - 1,)),
        ],
        compiler_params=pltpu.CompilerParams(
            collective_id=0, has_side_effects=True, vmem_limit_bytes=22 * 1024 * 1024),
    )(*(pltpu.with_memory_space_constraint(x, pltpu.HBM)
        for x in (anchor, replica, projection, momentum.reshape(rows, rank))))
    new_params, new_mom = pl.pallas_call(
        functools.partial(apply_kernel, matrices, float(rows_dev * n_fsdp * rank)),
        out_shape=(
            jax.ShapeDtypeStruct((rows, width), BF16),
            jax.ShapeDtypeStruct((rows, rank), F32),
        ),
        in_specs=[vmem] * 6 + [smem] * 3,
        out_specs=(any_spec, any_spec),
        scratch_shapes=[
            pltpu.VMEM((3, size, width), BF16),
            pltpu.VMEM((matrices, 128), F32),
            dma((3,)), dma(()),
        ],
        compiler_params=pltpu.CompilerParams(vmem_limit_bytes=16 * 1024 * 1024),
    )(*(pltpu.with_memory_space_constraint(x, pltpu.VMEM) for x in held),
      rate_table, owner_list, layer_kind.T)
    return new_params.reshape(anchor_params.shape), new_mom.reshape(momentum.shape)


def solution(mesh):
    placed = (
        P(None, "fsdp", None),
        P("replica", None, "fsdp", None),
        P(),
        P(None, "fsdp", None),
        P(),
        P(),
        P(),
    )
    return jax.shard_map(
        local,
        mesh=mesh,
        in_specs=placed,
        out_specs=(P(None, "fsdp", None), P(None, "fsdp", None)),
        check_vma=False,
    )
```
